32 devices in a mesh: parts: 2 (over x), ff: 16 (over z, y, core).
Axes of the slice: x: 2, y: 2, z: 4, core: 2. Of those that a mesh axis runs over, the one named last changes fastest.
Arguments:
- tokens: bfloat16 [512, 8192], P(('parts', 'ff')), parts along dimension 0, may hold values from -6 to 6
- gate_weight: bfloat16 [8192, 14784], P(None, 'ff'), may hold values from -0.0625 to 0.0625
- up_weight: bfloat16 [8192, 14784], P(None, 'ff'), may hold values from -0.0625 to 0.0625
- test_matrix: bfloat16 [14784, 256], P('ff'), may hold values from -0.046875 to 0.046875
Outputs:
- factor: float32 [14784, 512], P('ff', 'parts'), parts along dimension 1
The draws below stay inside these ranges and needn't reach their ends.
There are 2 independent parts, one for each index of `parts`. The reference program is written for one: setup_inputs(seed, part) draws one part's arguments, and reference() takes and returns one part's arrays. A program takes and returns all parts, laid end to end along the dimension named above; an argument that names none is the same for every part. Nothing has to cross between parts.
All inputs are finite; a program needn't handle non-finite values.
Results may differ from the reference program's by a relative error of at most 0.015.
The reference program's roundings to bfloat16 on the way (of `key_rows` and `sketch_low`) count: a program that leaves them out, or rounds other values in their place, can miss the bound.
Values may be sent and summed in bfloat16 or wider, within the bound.
A program may use at most 128 MiB of HBM per device.

```python
import jax
import jax.numpy as jnp
from jax import lax

D = 8192
FFW = 14784
RANK = 256
TOKENS = 256


def block_levels(stream_key, extent, cuts, least, high):
    gain, own = 1.0, jax.random.fold_in(stream_key, 6)
    for dim, shards_of in cuts:
        steps = jnp.exp(jax.random.uniform(jax.random.fold_in(own, dim), (shards_of,), jnp.float32, least / len(cuts), high / len(cuts)))
        gain = gain * jnp.repeat(steps, extent[dim] // shards_of).reshape([-1 if axis == dim else 1 for axis in range(len(extent))])
    return gain


def gaussian(stream_key, extent, scale, limit, split=(), kind=jnp.bfloat16):
    result = jax.random.normal(stream_key, extent, jnp.float32) * scale
    if len(split) > 0:
        result = block_levels(stream_key, extent, split, -0.22, 0.18) * result
    return jnp.clip(result, min=-limit, max=limit).astype(kind)


def setup_inputs(seed: int = 0, part: int = 0) -> dict:
    streams_of = jax.random.split(jax.random.key(seed), 5)
    part_splits = jax.random.split(jax.random.fold_in(streams_of[4], part), 5)
    tokens = gaussian(part_splits[0], (TOKENS, D), 1.0, 6.0, ((0, 16),))
    gate_weight = gaussian(streams_of[1], (D, FFW), D ** -0.5, 0.0625, ((1, 16),))
    up_weight = gaussian(streams_of[2], (D, FFW), D ** -0.5, 0.0625, ((1, 16),))
    test_matrix = gaussian(streams_of[3], (FFW, RANK), FFW ** -0.5, 0.046875, ((0, 16),))
    return {"tokens": tokens, "gate_weight": gate_weight, "up_weight": up_weight, "test_matrix": test_matrix}


def reference(tokens, gate_weight, up_weight, test_matrix):
    gate_part = jnp.dot(tokens.astype(jnp.float32), gate_weight.astype(jnp.float32), preferred_element_type=jnp.float32)
    up_part = jnp.dot(tokens.astype(jnp.float32), up_weight.astype(jnp.float32), preferred_element_type=jnp.float32)
    key_rows = (jax.nn.silu(gate_part) * up_part).astype(jnp.bfloat16)
    sketch_rows = jnp.dot(key_rows.astype(jnp.float32), test_matrix.astype(jnp.float32), preferred_element_type=jnp.float32)
    sketch_low = sketch_rows.astype(jnp.bfloat16)
    sketch_y = jnp.dot(key_rows.T.astype(jnp.float32), sketch_low.astype(jnp.float32), preferred_element_type=jnp.float32)
    core_matrix = jnp.dot(sketch_rows.T, sketch_rows, precision=lax.Precision.HIGHEST)
    diag_shift = 0.1 * jnp.trace(core_matrix) / RANK
    core_matrix = core_matrix + diag_shift * jnp.eye(RANK, dtype=jnp.float32)
    chol_factor = jnp.linalg.cholesky(core_matrix)
    solved = jax.scipy.linalg.solve_triangular(chol_factor, sketch_y.T, lower=True)
    return solved.T
```

```python
import functools

import jax
import jax.numpy as jnp
from jax import lax
from jax.experimental import pallas as pl
from jax.experimental.pallas import tpu as pltpu
from jax.sharding import PartitionSpec as P

MESH = pl.DeviceIdType.MESH
CHUNKS = 4


def keys_kernel(n, tok_hbm, gate_hbm, up_hbm, test_ref, key_ref, sketch_ref,
                tok, gw, uw, gacc, uacc, part, sib_sum, half_sum, slices, full,
                loc_sem, w_sem, xs, xr, zs, zr, ys, yr, ss, sr,
                r0s, r0r, r1s, r1r, r2s, r2r, r3s, r3r):
    t, width = tok_hbm.shape
    kc = width // (2 * CHUNKS)
    chips, lines = n // 2, n // 4
    rows = n * t
    me = lax.axis_index("ff")
    core, chip = me % 2, me // 2
    b, a = chip % 2, chip // 2
    sibling = chip * 2 + (1 - core)

    def same_core(other_chip):
        return other_chip * 2 + core

    def line_chip(step, side):
        return ((a - step + lines) % lines) * 2 + side

    def send(src, dst, ssem, rsem, target):
        return pltpu.make_async_remote_copy(
            src_ref=src, dst_ref=dst, send_sem=ssem, recv_sem=rsem,
            device_id={"ff": target}, device_id_type=MESH)

    def own_copy(g):
        return pltpu.make_async_copy(
            tok_hbm.at[:, pl.ds(g * kc, kc)], tok.at[g, pl.ds(me * t, t), :], loc_sem.at[g])

    def gate_copy(g):
        return pltpu.make_async_copy(gate_hbm.at[pl.ds(g * kc, kc), :], gw.at[g], w_sem.at[0, g])

    def up_copy(g):
        return pltpu.make_async_copy(up_hbm.at[pl.ds(g * kc, kc), :], uw.at[g], w_sem.at[1, g])

    for i in range(CHUNKS):
        own_copy((1 - core) * CHUNKS + i).start()
    for i in range(CHUNKS):
        own_copy(core * CHUNKS + i).start()
    for i in range(CHUNKS):
        for h in (core, 1 - core):
            gate_copy(h * CHUNKS + i).start()
            up_copy(h * CHUNKS + i).start()

    barrier = pltpu.get_barrier_semaphore()
    pl.semaphore_signal(barrier, inc=1, device_id={"ff": sibling}, device_id_type=MESH)
    for d in range(1, chips):
        pl.semaphore_signal(barrier, inc=1, device_id={"ff": same_core((chip + d) % chips)}, device_id_type=MESH)
    pl.semaphore_wait(barrier, chips)

    def chip_rows(c):
        return pl.ds(pl.multiple_of(c * 2 * t, 2 * t), 2 * t)

    def pair_copy(g):
        own = tok.at[g, pl.ds(me * t, t), :]
        return send(own, own, xs.at[g], xr.at[g], sibling)

    def z_copy(i, d):
        block = tok.at[core * CHUNKS + i, chip_rows(chip), :]
        return send(block, block, zs.at[i, d], zr.at[i, d], same_core(((a + d) % lines) * 2 + b))

    def y_copy(i, d):
        block = tok.at[core * CHUNKS + i, chip_rows(line_chip(d, b)), :]
        return send(block, block, ys.at[i, d], yr.at[i, d], same_core(a * 2 + (1 - b)))

    def pass_copy(i, d, other):
        side = 1 - b if other else b
        block = tok.at[core * CHUNKS + i, chip_rows(line_chip(d, side)), :]
        return send(block, block, ss.at[i, other, d], sr.at[i, other, d], sibling)

    for i in range(CHUNKS):
        g = (1 - core) * CHUNKS + i
        own_copy(g).wait()
        pair_copy(g).start()
    for i in range(CHUNKS):
        g = core * CHUNKS + i
        own_copy(g).wait()
        pair_copy(g).start()
    for i in range(CHUNKS):
        pair_copy(core * CHUNKS + i).wait_recv()
        for d in range(1, lines):
            z_copy(i, d).start()
        y_copy(i, 0).start()

    gacc[...] = jnp.zeros_like(gacc)
    uacc[...] = jnp.zeros_like(uacc)

    def multiply(g):
        gate_copy(g).wait()
        up_copy(g).wait()
        gacc[...] += jnp.dot(tok[g], gw[g], preferred_element_type=jnp.float32)
        uacc[...] += jnp.dot(tok[g], uw[g], preferred_element_type=jnp.float32)

    def chunk(i, carry):
        for d in range(1, lines):
            z_copy(i, d).wait_recv()
            y_copy(i, d).start()
            pass_copy(i, d, 0).start()
        for d in range(lines):
            y_copy(i, d).wait_recv()
            pass_copy(i, d, 1).start()

        def halves(k, carry):
            h = (core + k) % 2

            @pl.when(k == 1)
            def _():
                pair_copy((1 - core) * CHUNKS + i).wait_recv()
                for d in range(lines):
                    if d > 0:
                        pass_copy(i, d, 0).wait_recv()
                    pass_copy(i, d, 1).wait_recv()

            multiply(h * CHUNKS + i)
            return carry

        return lax.fori_loop(0, 2, halves, carry)

    lax.fori_loop(0, CHUNKS, chunk, 0)

    gate = gacc[...]
    keys = (gate / (1.0 + jnp.exp(-gate)) * uacc[...]).astype(jnp.bfloat16)
    key_ref[...] = keys
    part[...] = jnp.dot(keys, test_ref[...], preferred_element_type=jnp.float32)

    half = rows // 2
    pair = send(part.at[pl.ds((1 - core) * half, half), :], sib_sum, r0s, r0r, sibling)
    pair.start()
    pair.wait_recv()
    half_sum[...] = part[pl.ds(core * half, half), :] + sib_sum[...]

    def slice_copy(d):
        target = (chip + d) % chips
        return send(half_sum.at[pl.ds(target * t, t), :], slices.at[d], r1s.at[d], r1r.at[d], same_core(target))

    for d in range(1, chips):
        slice_copy(d).start()
    total = half_sum[pl.ds(chip * t, t), :]
    for d in range(1, chips):
        slice_copy(d).wait_recv()
        total = total + slices[d]
    full[pl.ds(core * half + chip * t, t), :] = total

    def back_copy(d):
        own = full.at[pl.ds(core * half + chip * t, t), :]
        return send(own, own, r2s.at[d], r2r.at[d], same_core((chip + d) % chips))

    def back_pass(d):
        block = full.at[pl.ds(core * half + ((chip - d + chips) % chips) * t, t), :]
        return send(block, block, r3s.at[d], r3r.at[d], sibling)

    for d in range(1, chips):
        back_copy(d).start()
    back_pass(0).start()
    for d in range(1, chips):
        back_copy(d).wait_recv()
        back_pass(d).start()
    for d in range(chips):
        back_pass(d).wait_recv()
    sketch_ref[...] = full[...]

    def drain(i, carry):
        pair_copy(i).wait_send()
        pair_copy(CHUNKS + i).wait_send()
        for d in range(lines):
            if d > 0:
                z_copy(i, d).wait_send()
                pass_copy(i, d, 0).wait_send()
            y_copy(i, d).wait_send()
            pass_copy(i, d, 1).wait_send()
        return carry

    lax.fori_loop(0, CHUNKS, drain, 0)
    pair.wait_send()
    for d in range(1, chips):
        slice_copy(d).wait_send()
        back_copy(d).wait_send()
    for d in range(chips):
        back_pass(d).wait_send()


def keys_and_sketch(n, tokens, gate_weight, up_weight, test_matrix):
    t, width = tokens.shape
    hidden = gate_weight.shape[1]
    rank = test_matrix.shape[1]
    rows, kc = n * t, width // (2 * CHUNKS)
    chips, lines = n // 2, n // 4
    vmem, dma = pltpu.VMEM, pltpu.SemaphoreType.DMA
    f32, bf16 = jnp.float32, jnp.bfloat16
    return pl.pallas_call(
        functools.partial(keys_kernel, n),
        out_shape=(jax.ShapeDtypeStruct((rows, hidden), bf16), jax.ShapeDtypeStruct((rows, rank), f32)),
        in_specs=[pl.BlockSpec(memory_space=pl.ANY)] * 3 + [pl.BlockSpec(memory_space=pltpu.VMEM)],
        out_specs=(pl.BlockSpec(memory_space=pltpu.VMEM),) * 2,
        scratch_shapes=[
            vmem((2 * CHUNKS, rows, kc), bf16),
            vmem((2 * CHUNKS, kc, hidden), bf16),
            vmem((2 * CHUNKS, kc, hidden), bf16),
            vmem((rows, hidden), f32),
            vmem((rows, hidden), f32),
            vmem((rows, rank), f32),
            vmem((rows // 2, rank), f32),
            vmem((rows // 2, rank), f32),
            vmem((chips, t, rank), f32),
            vmem((rows, rank), f32),
            dma((2 * CHUNKS,)),
            dma((2, 2 * CHUNKS)),
            dma((2 * CHUNKS,)), dma((2 * CHUNKS,)),
            dma((CHUNKS, lines)), dma((CHUNKS, lines)),
            dma((CHUNKS, lines)), dma((CHUNKS, lines)),
            dma((CHUNKS, 2, lines)), dma((CHUNKS, 2, lines)),
            dma, dma,
            dma((chips,)), dma((chips,)),
            dma((chips,)), dma((chips,)),
            dma((chips,)), dma((chips,)),
        ],
        compiler_params=pltpu.CompilerParams(
            collective_id=0, has_side_effects=True, vmem_limit_bytes=56 * 2**20),
    )(tokens, gate_weight, up_weight, test_matrix)


def solution(mesh):
    n = mesh.shape["ff"]

    def per_device(tokens, gate_weight, up_weight, test_matrix):
        key_rows, sketch_rows = keys_and_sketch(n, tokens, gate_weight, up_weight, test_matrix)
        core_matrix = jnp.dot(sketch_rows.T, sketch_rows, precision=lax.Precision.HIGHEST)
        sketch_low = sketch_rows.astype(jnp.bfloat16)
        sketch_y = jnp.dot(key_rows.T, sketch_low, preferred_element_type=jnp.float32)
        rank_width = core_matrix.shape[0]
        diag_shift = 0.1 * jnp.trace(core_matrix) / rank_width
        core_matrix = core_matrix + diag_shift * jnp.eye(rank_width, dtype=jnp.float32)
        chol_factor = jnp.linalg.cholesky(core_matrix)
        solved = jax.scipy.linalg.solve_triangular(chol_factor, sketch_y.T, lower=True)
        return solved.T

    placed = (P(("parts", "ff"), None), P(None, "ff"), P(None, "ff"), P("ff", None))
    return jax.shard_map(
        per_device, mesh=mesh, in_specs=placed, out_specs=P("ff", "parts"), check_vma=False
    )
```

```python
import functools

import jax
import jax.numpy as jnp
from jax import lax
from jax.experimental import pallas as pl
from jax.experimental.pallas import tpu as pltpu
from jax.sharding import PartitionSpec as P

MESH = pl.DeviceIdType.MESH
CHUNKS = 4


def contract(x, y, x_dim, y_dim, precision=None):
    return lax.dot_general(x, y, (((x_dim,), (y_dim,)), ((), ())), precision=precision,
                           preferred_element_type=jnp.float32)


def keys_kernel(n, tok_hbm, gate_hbm, up_hbm, test_ref, key_ref, sketch_ref,
                tok, gw, uw, gacc, uacc, part, sib_sum, half_sum, slices, full,
                loc_sem, w_sem, xs, xr, zs, zr, ys, yr, ss, sr,
                r0s, r0r, r1s, r1r, r2s, r2r, r3s, r3r):
    t, width = tok_hbm.shape
    kc = width // (2 * CHUNKS)
    chips, lines = n // 2, n // 4
    rows = n * t
    me = lax.axis_index("ff")
    core, chip = me % 2, me // 2
    b, a = chip % 2, chip // 2
    sibling = chip * 2 + (1 - core)

    def same_core(other_chip):
        return other_chip * 2 + core

    def line_chip(step, side):
        return ((a - step + lines) % lines) * 2 + side

    def send(src, dst, ssem, rsem, target):
        return pltpu.make_async_remote_copy(
            src_ref=src, dst_ref=dst, send_sem=ssem, recv_sem=rsem,
            device_id={"ff": target}, device_id_type=MESH)

    def own_copy(g):
        return pltpu.make_async_copy(
            tok_hbm.at[:, pl.ds(g * kc, kc)], tok.at[g, pl.ds(me * t, t), :], loc_sem.at[g])

    def gate_copy(g):
        return pltpu.make_async_copy(gate_hbm.at[:, pl.ds(g * kc, kc)], gw.at[g], w_sem.at[0, g])

    def up_copy(g):
        return pltpu.make_async_copy(up_hbm.at[:, pl.ds(g * kc, kc)], uw.at[g], w_sem.at[1, g])

    for i in range(CHUNKS):
        own_copy((1 - core) * CHUNKS + i).start()
    for i in range(CHUNKS):
        own_copy(core * CHUNKS + i).start()
    for i in range(CHUNKS):
        for h in (core, 1 - core):
            gate_copy(h * CHUNKS + i).start()
            up_copy(h * CHUNKS + i).start()

    barrier = pltpu.get_barrier_semaphore()
    pl.semaphore_signal(barrier, inc=1, device_id={"ff": sibling}, device_id_type=MESH)
    for d in range(1, chips):
        pl.semaphore_signal(barrier, inc=1, device_id={"ff": same_core((chip + d) % chips)}, device_id_type=MESH)
    pl.semaphore_wait(barrier, chips)

    def chip_rows(c):
        return pl.ds(pl.multiple_of(c * 2 * t, 2 * t), 2 * t)

    def pair_copy(g):
        own = tok.at[g, pl.ds(me * t, t), :]
        return send(own, own, xs.at[g], xr.at[g], sibling)

    def z_copy(i, d):
        block = tok.at[core * CHUNKS + i, chip_rows(chip), :]
        return send(block, block, zs.at[i, d], zr.at[i, d], same_core(((a + d) % lines) * 2 + b))

    def y_copy(i, d):
        block = tok.at[core * CHUNKS + i, chip_rows(line_chip(d, b)), :]
        return send(block, block, ys.at[i, d], yr.at[i, d], same_core(a * 2 + (1 - b)))

    def pass_copy(i, d, other):
        side = 1 - b if other else b
        block = tok.at[core * CHUNKS + i, chip_rows(line_chip(d, side)), :]
        return send(block, block, ss.at[i, other, d], sr.at[i, other, d], sibling)

    for i in range(CHUNKS):
        g = (1 - core) * CHUNKS + i
        own_copy(g).wait()
        pair_copy(g).start()
    for i in range(CHUNKS):
        g = core * CHUNKS + i
        own_copy(g).wait()
        pair_copy(g).start()
    for i in range(CHUNKS):
        pair_copy(core * CHUNKS + i).wait_recv()
        for d in range(1, lines):
            z_copy(i, d).start()
        y_copy(i, 0).start()

    gacc[...] = jnp.zeros_like(gacc)
    uacc[...] = jnp.zeros_like(uacc)

    def multiply(g):
        gate_copy(g).wait()
        up_copy(g).wait()
        block = tok[g]
        gacc[...] += contract(gw[g], block, 1, 1)
        uacc[...] += contract(uw[g], block, 1, 1)

    def chunk(i, carry):
        for d in range(1, lines):
            z_copy(i, d).wait_recv()
            y_copy(i, d).start()
            pass_copy(i, d, 0).start()
        for d in range(lines):
            y_copy(i, d).wait_recv()
            pass_copy(i, d, 1).start()

        def halves(k, carry):
            h = (core + k) % 2

            @pl.when(k == 1)
            def _():
                pair_copy((1 - core) * CHUNKS + i).wait_recv()
                for d in range(lines):
                    if d > 0:
                        pass_copy(i, d, 0).wait_recv()
                    pass_copy(i, d, 1).wait_recv()

            multiply(h * CHUNKS + i)
            return carry

        return lax.fori_loop(0, 2, halves, carry)

    lax.fori_loop(0, CHUNKS, chunk, 0)

    gate = gacc[...]
    keys = (gate / (1.0 + jnp.exp(-gate)) * uacc[...]).astype(jnp.bfloat16)
    key_ref[...] = keys
    part[...] = contract(keys, test_ref[...], 0, 0)

    half = rows // 2
    pair = send(part.at[pl.ds((1 - core) * half, half), :], sib_sum, r0s, r0r, sibling)
    pair.start()
    pair.wait_recv()
    half_sum[...] = part[pl.ds(core * half, half), :] + sib_sum[...]

    def slice_copy(d):
        target = (chip + d) % chips
        return send(half_sum.at[pl.ds(target * t, t), :], slices.at[d], r1s.at[d], r1r.at[d], same_core(target))

    for d in range(1, chips):
        slice_copy(d).start()
    total = half_sum[pl.ds(chip * t, t), :]
    for d in range(1, chips):
        slice_copy(d).wait_recv()
        total = total + slices[d]
    full[pl.ds(core * half + chip * t, t), :] = total

    def back_copy(d):
        own = full.at[pl.ds(core * half + chip * t, t), :]
        return send(own, own, r2s.at[d], r2r.at[d], same_core((chip + d) % chips))

    def back_pass(d):
        block = full.at[pl.ds(core * half + ((chip - d + chips) % chips) * t, t), :]
        return send(block, block, r3s.at[d], r3r.at[d], sibling)

    for d in range(1, chips):
        back_copy(d).start()
    back_pass(0).start()
    for d in range(1, chips):
        back_copy(d).wait_recv()
        back_pass(d).start()
    for d in range(chips):
        back_pass(d).wait_recv()
    sketch_ref[...] = full[...]

    def drain(i, carry):
        pair_copy(i).wait_send()
        pair_copy(CHUNKS + i).wait_send()
        for d in range(lines):
            if d > 0:
                z_copy(i, d).wait_send()
                pass_copy(i, d, 0).wait_send()
            y_copy(i, d).wait_send()
            pass_copy(i, d, 1).wait_send()
        return carry

    lax.fori_loop(0, CHUNKS, drain, 0)
    pair.wait_send()
    for d in range(1, chips):
        slice_copy(d).wait_send()
        back_copy(d).wait_send()
    for d in range(chips):
        back_pass(d).wait_send()


def keys_and_sketch(n, tokens, gate_weight, up_weight, test_matrix):
    t, width = tokens.shape
    hidden = gate_weight.shape[0]
    rank = test_matrix.shape[1]
    rows, kc = n * t, width // (2 * CHUNKS)
    chips, lines = n // 2, n // 4
    vmem, dma = pltpu.VMEM, pltpu.SemaphoreType.DMA
    f32, bf16 = jnp.float32, jnp.bfloat16
    return pl.pallas_call(
        functools.partial(keys_kernel, n),
        out_shape=(jax.ShapeDtypeStruct((hidden, rows), bf16), jax.ShapeDtypeStruct((rows, rank), f32)),
        in_specs=[pl.BlockSpec(memory_space=pl.ANY)] * 3 + [pl.BlockSpec(memory_space=pltpu.VMEM)],
        out_specs=(pl.BlockSpec(memory_space=pltpu.VMEM),) * 2,
        scratch_shapes=[
            vmem((2 * CHUNKS, rows, kc), bf16),
            vmem((2 * CHUNKS, hidden, kc), bf16),
            vmem((2 * CHUNKS, hidden, kc), bf16),
            vmem((hidden, rows), f32),
            vmem((hidden, rows), f32),
            vmem((rows, rank), f32),
            vmem((rows // 2, rank), f32),
            vmem((rows // 2, rank), f32),
            vmem((chips, t, rank), f32),
            vmem((rows, rank), f32),
            dma((2 * CHUNKS,)),
            dma((2, 2 * CHUNKS)),
            dma((2 * CHUNKS,)), dma((2 * CHUNKS,)),
            dma((CHUNKS, lines)), dma((CHUNKS, lines)),
            dma((CHUNKS, lines)), dma((CHUNKS, lines)),
            dma((CHUNKS, 2, lines)), dma((CHUNKS, 2, lines)),
            dma, dma,
            dma((chips,)), dma((chips,)),
            dma((chips,)), dma((chips,)),
            dma((chips,)), dma((chips,)),
        ],
        compiler_params=pltpu.CompilerParams(
            collective_id=0, has_side_effects=True, vmem_limit_bytes=56 * 2**20),
    )(tokens, gate_weight, up_weight, test_matrix)


def solution(mesh):
    n = mesh.shape["ff"]

    def per_device(tokens, gate_weight, up_weight, test_matrix):
        key_rows, sketch_rows = keys_and_sketch(n, tokens, gate_weight.T, up_weight.T, test_matrix)
        core_matrix = jnp.dot(sketch_rows.T, sketch_rows, precision=lax.Precision.HIGHEST)
        sketch_low = sketch_rows.astype(jnp.bfloat16)
        sketch_y = jnp.dot(key_rows, sketch_low, preferred_element_type=jnp.float32)
        rank_width = core_matrix.shape[0]
        diag_shift = 0.1 * jnp.trace(core_matrix) / rank_width
        core_matrix = core_matrix + diag_shift * jnp.eye(rank_width, dtype=jnp.float32)
        chol_factor = jnp.linalg.cholesky(core_matrix)
        solved = jax.scipy.linalg.solve_triangular(chol_factor, sketch_y.T, lower=True)
        return solved.T

    placed = (P(("parts", "ff"), None), P(None, "ff"), P(None, "ff"), P("ff", None))
    return jax.shard_map(
        per_device, mesh=mesh, in_specs=placed, out_specs=P("ff", "parts"), check_vma=False
    )
```

```python
import functools

import jax
import jax.numpy as jnp
from jax import lax
from jax.experimental import pallas as pl
from jax.experimental.pallas import tpu as pltpu
from jax.sharding import PartitionSpec as P

MESH = pl.DeviceIdType.MESH
CHUNKS = 4


def contract(x, y, x_dim, y_dim, precision=None):
    return lax.dot_general(x, y, (((x_dim,), (y_dim,)), ((), ())), precision=precision,
                           preferred_element_type=jnp.float32)


def keys_kernel(n, tok_hbm, gate_hbm, up_hbm, test_ref, key_ref, sketch_ref,
                tok, gw, uw, gacc, uacc, part, sib_sum, half_sum, slices, full,
                loc_sem, w_sem, xs, xr, zs, zr, ys, yr, ss, sr,
                r0s, r0r, r1s, r1r, r2s, r2r, r3s, r3r):
    t, width = tok_hbm.shape
    kc = width // (2 * CHUNKS)
    chips, lines = n // 2, n // 4
    rows = n * t
    me = lax.axis_index("ff")
    core, chip = me % 2, me // 2
    b, a = chip % 2, chip // 2
    sibling = chip * 2 + (1 - core)

    def same_core(other_chip):
        return other_chip * 2 + core

    def line_chip(step, side):
        return ((a - step + lines) % lines) * 2 + side

    def send(src, dst, ssem, rsem, target):
        return pltpu.make_async_remote_copy(
            src_ref=src, dst_ref=dst, send_sem=ssem, recv_sem=rsem,
            device_id={"ff": target}, device_id_type=MESH)

    def own_copy(g):
        return pltpu.make_async_copy(
            tok_hbm.at[:, pl.ds(g * kc, kc)], tok.at[g, pl.ds(me * t, t), :], loc_sem.at[g])

    def gate_copy(g):
        return pltpu.make_async_copy(gate_hbm.at[:, pl.ds(g * kc, kc)], gw.at[g], w_sem.at[0, g])

    def up_copy(g):
        return pltpu.make_async_copy(up_hbm.at[:, pl.ds(g * kc, kc)], uw.at[g], w_sem.at[1, g])

    for i in range(CHUNKS):
        own_copy((1 - core) * CHUNKS + i).start()
    for i in range(CHUNKS):
        own_copy(core * CHUNKS + i).start()
    for i in range(CHUNKS):
        for h in (core, 1 - core):
            gate_copy(h * CHUNKS + i).start()
            up_copy(h * CHUNKS + i).start()

    barrier = pltpu.get_barrier_semaphore()
    pl.semaphore_signal(barrier, inc=1, device_id={"ff": sibling}, device_id_type=MESH)
    for d in range(1, chips):
        pl.semaphore_signal(barrier, inc=1, device_id={"ff": same_core((chip + d) % chips)}, device_id_type=MESH)
    pl.semaphore_wait(barrier, chips)

    def chip_rows(c):
        return pl.ds(pl.multiple_of(c * 2 * t, 2 * t), 2 * t)

    def pair_copy(g):
        own = tok.at[g, pl.ds(me * t, t), :]
        return send(own, own, xs.at[g], xr.at[g], sibling)

    def z_copy(i, d):
        block = tok.at[core * CHUNKS + i, chip_rows(chip), :]
        return send(block, block, zs.at[i, d], zr.at[i, d], same_core(((a + d) % lines) * 2 + b))

    def y_copy(i, d):
        block = tok.at[core * CHUNKS + i, chip_rows(line_chip(d, b)), :]
        return send(block, block, ys.at[i, d], yr.at[i, d], same_core(a * 2 + (1 - b)))

    def pass_copy(i, d, other):
        side = 1 - b if other else b
        block = tok.at[core * CHUNKS + i, chip_rows(line_chip(d, side)), :]
        return send(block, block, ss.at[i, other, d], sr.at[i, other, d], sibling)

    for i in range(CHUNKS):
        g = (1 - core) * CHUNKS + i
        own_copy(g).wait()
        pair_copy(g).start()
    for i in range(CHUNKS):
        g = core * CHUNKS + i
        own_copy(g).wait()
        pair_copy(g).start()
    for i in range(CHUNKS):
        pair_copy(core * CHUNKS + i).wait_recv()
        for d in range(1, lines):
            z_copy(i, d).start()
        y_copy(i, 0).start()

    gacc[...] = jnp.zeros_like(gacc)
    uacc[...] = jnp.zeros_like(uacc)

    def multiply(g):
        gate_copy(g).wait()
        up_copy(g).wait()
        block = tok[g]
        gacc[...] += contract(gw[g], block, 1, 1)
        uacc[...] += contract(uw[g], block, 1, 1)

    def chunk(i, carry):
        for d in range(1, lines):
            z_copy(i, d).wait_recv()
            y_copy(i, d).start()
            pass_copy(i, d, 0).start()
        for d in range(lines):
            y_copy(i, d).wait_recv()
            pass_copy(i, d, 1).start()

        def halves(k, carry):
            h = (core + k) % 2

            @pl.when(k == 1)
            def _():
                pair_copy((1 - core) * CHUNKS + i).wait_recv()
                for d in range(lines):
                    if d > 0:
                        pass_copy(i, d, 0).wait_recv()
                    pass_copy(i, d, 1).wait_recv()

            multiply(h * CHUNKS + i)
            return carry

        return lax.fori_loop(0, 2, halves, carry)

    lax.fori_loop(0, CHUNKS, chunk, 0)

    gate = gacc[...]
    keys = (gate / (1.0 + jnp.exp(-gate)) * uacc[...]).astype(jnp.bfloat16)
    key_ref[...] = keys
    part[...] = contract(keys, test_ref[...], 0, 0)

    half = rows // 2
    pair = send(part.at[pl.ds((1 - core) * half, half), :], sib_sum, r0s, r0r, sibling)
    pair.start()
    pair.wait_recv()
    half_sum[...] = part[pl.ds(core * half, half), :] + sib_sum[...]

    def slice_copy(d):
        target = (chip + d) % chips
        return send(half_sum.at[pl.ds(target * t, t), :], slices.at[d], r1s.at[d], r1r.at[d], same_core(target))

    for d in range(1, chips):
        slice_copy(d).start()
    total = half_sum[pl.ds(chip * t, t), :]
    for d in range(1, chips):
        slice_copy(d).wait_recv()
        total = total + slices[d]
    full[pl.ds(core * half + chip * t, t), :] = total

    def back_copy(d):
        own = full.at[pl.ds(core * half + chip * t, t), :]
        return send(own, own, r2s.at[d], r2r.at[d], same_core((chip + d) % chips))

    def back_pass(d):
        block = full.at[pl.ds(core * half + ((chip - d + chips) % chips) * t, t), :]
        return send(block, block, r3s.at[d], r3r.at[d], sibling)

    for d in range(1, chips):
        back_copy(d).start()
    back_pass(0).start()
    for d in range(1, chips):
        back_copy(d).wait_recv()
        back_pass(d).start()
    for d in range(chips):
        back_pass(d).wait_recv()
    sketch_ref[...] = full[...]

    def drain(i, carry):
        pair_copy(i).wait_send()
        pair_copy(CHUNKS + i).wait_send()
        for d in range(lines):
            if d > 0:
                z_copy(i, d).wait_send()
                pass_copy(i, d, 0).wait_send()
            y_copy(i, d).wait_send()
            pass_copy(i, d, 1).wait_send()
        return carry

    lax.fori_loop(0, CHUNKS, drain, 0)
    pair.wait_send()
    for d in range(1, chips):
        slice_copy(d).wait_send()
        back_copy(d).wait_send()
    for d in range(chips):
        back_pass(d).wait_send()


def keys_and_sketch(n, tokens, gate_weight, up_weight, test_matrix):
    t, width = tokens.shape
    hidden = gate_weight.shape[0]
    rank = test_matrix.shape[1]
    rows, kc = n * t, width // (2 * CHUNKS)
    chips, lines = n // 2, n // 4
    vmem, dma = pltpu.VMEM, pltpu.SemaphoreType.DMA
    f32, bf16 = jnp.float32, jnp.bfloat16
    return pl.pallas_call(
        functools.partial(keys_kernel, n),
        out_shape=(jax.ShapeDtypeStruct((hidden, rows), bf16), jax.ShapeDtypeStruct((rows, rank), f32)),
        in_specs=[pl.BlockSpec(memory_space=pl.ANY)] * 3 + [pl.BlockSpec(memory_space=pltpu.VMEM)],
        out_specs=(pl.BlockSpec(memory_space=pltpu.VMEM),) * 2,
        scratch_shapes=[
            vmem((2 * CHUNKS, rows, kc), bf16),
            vmem((2 * CHUNKS, hidden, kc), bf16),
            vmem((2 * CHUNKS, hidden, kc), bf16),
            vmem((hidden, rows), f32),
            vmem((hidden, rows), f32),
            vmem((rows, rank), f32),
            vmem((rows // 2, rank), f32),
            vmem((rows // 2, rank), f32),
            vmem((chips, t, rank), f32),
            vmem((rows, rank), f32),
            dma((2 * CHUNKS,)),
            dma((2, 2 * CHUNKS)),
            dma((2 * CHUNKS,)), dma((2 * CHUNKS,)),
            dma((CHUNKS, lines)), dma((CHUNKS, lines)),
            dma((CHUNKS, lines)), dma((CHUNKS, lines)),
            dma((CHUNKS, 2, lines)), dma((CHUNKS, 2, lines)),
            dma, dma,
            dma((chips,)), dma((chips,)),
            dma((chips,)), dma((chips,)),
            dma((chips,)), dma((chips,)),
        ],
        compiler_params=pltpu.CompilerParams(
            collective_id=0, has_side_effects=True, vmem_limit_bytes=56 * 2**20),
    )(tokens, gate_weight, up_weight, test_matrix)


def factor_kernel(key_ref, sketch_ref, out_ref, work):
    rank = out_ref.shape[1]
    span = work.shape[1]
    tile, step = 128, 8
    sketch = sketch_ref[...]
    core_matrix = contract(sketch, sketch, 0, 0, lax.Precision.HIGHEST)
    diag = (lax.broadcasted_iota(jnp.int32, (rank, rank), 0)
            == lax.broadcasted_iota(jnp.int32, (rank, rank), 1))
    shift = 0.1 * jnp.sum(jnp.where(diag, core_matrix, 0.0)) / rank
    work[:, :rank] = core_matrix + jnp.where(diag, shift, 0.0)
    work[:, rank:] = sketch.astype(jnp.bfloat16).astype(jnp.float32).T
    row_id = lax.broadcasted_iota(jnp.int32, (step, tile), 0)

    for k in range(0, rank, step):
        first = k // tile * tile
        head = work[k:k + step, first:first + tile]
        a = [[jnp.broadcast_to(head[i:i + 1, k - first + j:k - first + j + 1], (step, tile))
              for j in range(i + 1)] for i in range(step)]
        low = [[None] * step for _ in range(step)]
        inv = [[None] * step for _ in range(step)]
        for j in range(step):
            inv[j][j] = lax.rsqrt(a[j][j])
            for i in range(j + 1, step):
                low[i][j] = a[i][j] * inv[j][j]
            for i in range(j + 1, step):
                for m in range(j + 1, i + 1):
                    a[i][m] = a[i][m] - low[i][j] * low[m][j]
        for j in range(step):
            for i in range(j + 1, step):
                total = low[i][j] * inv[j][j]
                for m in range(j + 1, i):
                    total = total + low[i][m] * inv[m][j]
                inv[i][j] = -inv[i][i] * total
        columns = []
        for j in range(step):
            column = jnp.zeros((step, tile), jnp.float32)
            for i in range(j, step):
                column = jnp.where(row_id == i, inv[i][j], column)
            columns.append(column)
        tiles = []
        for c in range(first, span, tile):
            block = head if c == first else work[k:k + step, c:c + tile]
            total = columns[0] * block[0:1, :]
            for j in range(1, step):
                total = total + columns[j] * block[j:j + 1, :]
            if c >= rank:
                work[k:k + step, c:c + tile] = total
            tiles.append(total)
        if k + step < rank:
            solved = jnp.concatenate(tiles, axis=1)
            turned = solved[:, :rank - first].T[k + step - first:, :]
            work[k + step:, first:] -= contract(turned, solved, 1, 0, lax.Precision.HIGHEST)
    basis = work[:, rank:]
    high = basis.astype(jnp.bfloat16)
    rest = (basis - high.astype(jnp.float32)).astype(jnp.bfloat16)
    keys = key_ref[...]
    out_ref[...] = contract(keys, high, 1, 1) + contract(keys, rest, 1, 1)


def factor_of(key_rows, sketch_rows):
    hidden, rows = key_rows.shape
    rank = sketch_rows.shape[1]
    return pl.pallas_call(
        factor_kernel,
        out_shape=jax.ShapeDtypeStruct((hidden, rank), jnp.float32),
        in_specs=[pl.BlockSpec(memory_space=pltpu.VMEM)] * 2,
        out_specs=pl.BlockSpec(memory_space=pltpu.VMEM),
        scratch_shapes=[pltpu.VMEM((rank, rank + rows), jnp.float32)],
        compiler_params=pltpu.CompilerParams(vmem_limit_bytes=32 * 2**20),
    )(key_rows, sketch_rows)


def solution(mesh):
    n = mesh.shape["ff"]

    def per_device(tokens, gate_weight, up_weight, test_matrix):
        key_rows, sketch_rows = keys_and_sketch(n, tokens, gate_weight.T, up_weight.T, test_matrix)
        return factor_of(key_rows, sketch_rows)

    placed = (P(("parts", "ff"), None), P(None, "ff"), P(None, "ff"), P("ff", None))
    return jax.shard_map(
        per_device, mesh=mesh, in_specs=placed, out_specs=P("ff", "parts"), check_vma=False
    )
```

```python
import functools

import jax
import jax.numpy as jnp
from jax import lax
from jax.experimental import pallas as pl
from jax.experimental.pallas import tpu as pltpu
from jax.sharding import PartitionSpec as P

MESH = pl.DeviceIdType.MESH
CHUNKS = 4
AHEAD = 1


def contract(x, y, x_dim, y_dim, precision=None):
    return lax.dot_general(x, y, (((x_dim,), (y_dim,)), ((), ())), precision=precision,
                           preferred_element_type=jnp.float32)


def keys_kernel(n, tok_hbm, gate_hbm, up_hbm, test_ref, key_ref, sketch_ref,
                stage, tok, gw, uw, gacc, uacc, part, sib_sum, half_sum, slices, full,
                loc_sem, w_sem, xs, xr, zs, zr, ys, yr, ss, sr,
                r0s, r0r, r1s, r1r, r2s, r2r, r3s, r3r):
    t, width = tok_hbm.shape
    kc = width // (2 * CHUNKS)
    chips, lines = n // 2, n // 4
    rows, half = n * t, n * t // 2
    me = lax.axis_index("ff")
    core, chip = me % 2, me // 2
    b, a = chip % 2, chip // 2
    sibling = chip * 2 + (1 - core)

    def same_core(other_chip):
        return other_chip * 2 + core

    def send(src, dst, ssem, rsem, target):
        return pltpu.make_async_remote_copy(
            src_ref=src, dst_ref=dst, send_sem=ssem, recv_sem=rsem,
            device_id={"ff": target}, device_id_type=MESH)

    def chip_rows(place, side):
        return pl.ds(pl.multiple_of((side * lines + place) * 2 * t, 2 * t), 2 * t)

    own_rows = pl.ds(pl.multiple_of(((b * lines + a) * 2 + core) * t, t), t)

    def own_copy(i):
        g = core * CHUNKS + i
        return pltpu.make_async_copy(tok_hbm.at[:, pl.ds(g * kc, kc)], tok.at[g, own_rows, :], loc_sem.at[0, i])

    def stage_copy(i):
        g = (1 - core) * CHUNKS + i
        return pltpu.make_async_copy(tok_hbm.at[:, pl.ds(g * kc, kc)], stage.at[i], loc_sem.at[1, i])

    def gate_copy(g):
        return pltpu.make_async_copy(gate_hbm.at[:, pl.ds(g * kc, kc)], gw.at[g], w_sem.at[0, g])

    def up_copy(g):
        return pltpu.make_async_copy(up_hbm.at[:, pl.ds(g * kc, kc)], uw.at[g], w_sem.at[1, g])

    for i in range(CHUNKS):
        stage_copy(i).start()
        own_copy(i).start()
    for i in range(CHUNKS):
        for h in (core, 1 - core):
            gate_copy(h * CHUNKS + i).start()
            up_copy(h * CHUNKS + i).start()

    barrier = pltpu.get_barrier_semaphore()
    pl.semaphore_signal(barrier, inc=1, device_id={"ff": sibling}, device_id_type=MESH)
    for d in range(1, chips):
        pl.semaphore_signal(barrier, inc=1, device_id={"ff": same_core((chip + d) % chips)}, device_id_type=MESH)
    pl.semaphore_wait(barrier, chips)

    def pair_copy(i):
        return send(stage.at[i], tok.at[(1 - core) * CHUNKS + i, own_rows, :], xs.at[i], xr.at[i], sibling)

    def z_copy(i, d):
        block = tok.at[core * CHUNKS + i, chip_rows(a, b), :]
        return send(block, block, zs.at[i, d], zr.at[i, d], same_core(((a + d) % lines) * 2 + b))

    def y_copy(i):
        line = tok.at[core * CHUNKS + i, pl.ds(pl.multiple_of(b * half, half), half), :]
        return send(line, line, ys.at[i], yr.at[i], same_core(a * 2 + (1 - b)))

    def pass_copy(i):
        block = tok.at[core * CHUNKS + i]
        return send(block, block, ss.at[i], sr.at[i], sibling)

    def cross(i):
        for d in range(1, lines):
            z_copy(i, d).wait_recv()
        y_copy(i).start()

        @pl.when(i + AHEAD < CHUNKS)
        def _():
            begin(i + AHEAD)

    for i in range(CHUNKS):
        stage_copy(i).wait()
        pair_copy(i).start()
    def begin(i):
        own_copy(i).wait()
        pair_copy(i).wait_recv()
        for d in range(1, lines):
            z_copy(i, d).start()

    for i in range(AHEAD):
        begin(i)

    gacc[...] = jnp.zeros_like(gacc)
    uacc[...] = jnp.zeros_like(uacc)

    def multiply(g):
        gate_copy(g).wait()
        up_copy(g).wait()
        block = tok[g]
        gacc[...] += contract(gw[g], block, 1, 1)
        uacc[...] += contract(uw[g], block, 1, 1)

    def chunk(i, carry):
        @pl.when(i + 1 < CHUNKS)
        def _():
            cross(i + 1)

        y_copy(i).wait_recv()
        pass_copy(i).start()

        def halves(k, carry):
            @pl.when(k == 1)
            def _():
                pass_copy(i).wait_recv()

            multiply(((core + k) % 2) * CHUNKS + i)
            return carry

        return lax.fori_loop(0, 2, halves, carry)

    cross(jnp.int32(0))
    lax.fori_loop(0, CHUNKS, chunk, 0)

    gate = gacc[...]
    keys = (gate / (1.0 + jnp.exp(-gate)) * uacc[...]).astype(jnp.bfloat16)
    key_ref[...] = keys
    part[...] = contract(keys, test_ref[...], 0, 0)

    pair = send(part.at[pl.ds((1 - core) * half, half), :], sib_sum, r0s, r0r, sibling)
    pair.start()
    pair.wait_recv()
    half_sum[...] = part[pl.ds(core * half, half), :] + sib_sum[...]

    def slice_copy(d):
        target = (chip + d) % chips
        return send(half_sum.at[pl.ds(target * t, t), :], slices.at[d], r1s.at[d], r1r.at[d], same_core(target))

    for d in range(1, chips):
        slice_copy(d).start()
    total = half_sum[pl.ds(chip * t, t), :]
    for d in range(1, chips):
        slice_copy(d).wait_recv()
        total = total + slices[d]
    full[pl.ds(core * half + chip * t, t), :] = total

    def back_copy(d):
        own = full.at[pl.ds(core * half + chip * t, t), :]
        return send(own, own, r2s.at[d], r2r.at[d], same_core((chip + d) % chips))

    def back_pass(d):
        block = full.at[pl.ds(core * half + ((chip - d + chips) % chips) * t, t), :]
        return send(block, block, r3s.at[d], r3r.at[d], sibling)

    for d in range(1, chips):
        back_copy(d).start()
    back_pass(0).start()
    for d in range(1, chips):
        back_copy(d).wait_recv()
        back_pass(d).start()
    for d in range(chips):
        back_pass(d).wait_recv()
    sketch_ref[...] = full[...]

    def drain(i, carry):
        pair_copy(i).wait_send()
        for d in range(1, lines):
            z_copy(i, d).wait_send()
        y_copy(i).wait_send()
        pass_copy(i).wait_send()
        return carry

    lax.fori_loop(0, CHUNKS, drain, 0)
    pair.wait_send()
    for d in range(1, chips):
        slice_copy(d).wait_send()
        back_copy(d).wait_send()
    for d in range(chips):
        back_pass(d).wait_send()


def keys_and_sketch(n, tokens, gate_weight, up_weight, test_matrix):
    t, width = tokens.shape
    hidden = gate_weight.shape[0]
    rank = test_matrix.shape[1]
    rows, kc = n * t, width // (2 * CHUNKS)
    chips, lines = n // 2, n // 4
    vmem, dma = pltpu.VMEM, pltpu.SemaphoreType.DMA
    f32, bf16 = jnp.float32, jnp.bfloat16
    return pl.pallas_call(
        functools.partial(keys_kernel, n),
        out_shape=(jax.ShapeDtypeStruct((hidden, rows), bf16), jax.ShapeDtypeStruct((rows, rank), f32)),
        in_specs=[pl.BlockSpec(memory_space=pl.ANY)] * 3 + [pl.BlockSpec(memory_space=pltpu.VMEM)],
        out_specs=(pl.BlockSpec(memory_space=pltpu.VMEM),) * 2,
        scratch_shapes=[
            vmem((CHUNKS, t, kc), bf16),
            vmem((2 * CHUNKS, rows, kc), bf16),
            vmem((2 * CHUNKS, hidden, kc), bf16),
            vmem((2 * CHUNKS, hidden, kc), bf16),
            vmem((hidden, rows), f32),
            vmem((hidden, rows), f32),
            vmem((rows, rank), f32),
            vmem((rows // 2, rank), f32),
            vmem((rows // 2, rank), f32),
            vmem((chips, t, rank), f32),
            vmem((rows, rank), f32),
            dma((2, CHUNKS)),
            dma((2, 2 * CHUNKS)),
            dma((CHUNKS,)), dma((CHUNKS,)),
            dma((CHUNKS, lines)), dma((CHUNKS, lines)),
            dma((CHUNKS,)), dma((CHUNKS,)),
            dma((CHUNKS,)), dma((CHUNKS,)),
            dma, dma,
            dma((chips,)), dma((chips,)),
            dma((chips,)), dma((chips,)),
            dma((chips,)), dma((chips,)),
        ],
        compiler_params=pltpu.CompilerParams(
            collective_id=0, has_side_effects=True, vmem_limit_bytes=56 * 2**20),
    )(tokens, gate_weight, up_weight, test_matrix)


def factor_kernel(key_hbm, sketch_ref, out_ref, work, key_ref, key_sem):
    load = pltpu.make_async_copy(key_hbm, key_ref, key_sem)
    load.start()
    rank = out_ref.shape[1]
    span = work.shape[1]
    tile, step = 128, 8
    sketch = sketch_ref[...]
    core_matrix = contract(sketch, sketch, 0, 0, lax.Precision.HIGHEST)
    diag = (lax.broadcasted_iota(jnp.int32, (rank, rank), 0)
            == lax.broadcasted_iota(jnp.int32, (rank, rank), 1))
    shift = 0.1 * jnp.sum(jnp.where(diag, core_matrix, 0.0)) / rank
    work[:, :rank] = core_matrix + jnp.where(diag, shift, 0.0)
    work[:, rank:] = sketch.astype(jnp.bfloat16).astype(jnp.float32).T
    row_id = lax.broadcasted_iota(jnp.int32, (step, tile), 0)

    for k in range(0, rank, step):
        first = k // tile * tile
        head = work[k:k + step, first:first + tile]
        a = [[jnp.broadcast_to(head[i:i + 1, k - first + j:k - first + j + 1], (step, tile))
              for j in range(i + 1)] for i in range(step)]
        low = [[None] * step for _ in range(step)]
        inv = [[None] * step for _ in range(step)]
        for j in range(step):
            inv[j][j] = lax.rsqrt(a[j][j])
            for i in range(j + 1, step):
                low[i][j] = a[i][j] * inv[j][j]
            for i in range(j + 1, step):
                for m in range(j + 1, i + 1):
                    a[i][m] = a[i][m] - low[i][j] * low[m][j]
        for j in range(step):
            for i in range(j + 1, step):
                total = low[i][j] * inv[j][j]
                for m in range(j + 1, i):
                    total = total + low[i][m] * inv[m][j]
                inv[i][j] = -inv[i][i] * total
        columns = []
        for j in range(step):
            column = jnp.zeros((step, tile), jnp.float32)
            for i in range(j, step):
                column = jnp.where(row_id == i, inv[i][j], column)
            columns.append(column)
        tiles = []
        for c in range(first, span, tile):
            block = head if c == first else work[k:k + step, c:c + tile]
            total = columns[0] * block[0:1, :]
            for j in range(1, step):
                total = total + columns[j] * block[j:j + 1, :]
            if c >= rank:
                work[k:k + step, c:c + tile] = total
            tiles.append(total)
        if k + step < rank:
            solved = jnp.concatenate(tiles, axis=1)
            turned = solved[:, :rank - first].T[k + step - first:, :]
            work[k + step:, first:] -= contract(turned, solved, 1, 0, lax.Precision.HIGHEST)
    basis = work[:, rank:]
    high = basis.astype(jnp.bfloat16)
    rest = (basis - high.astype(jnp.float32)).astype(jnp.bfloat16)
    load.wait()
    keys = key_ref[...]
    out_ref[...] = contract(keys, high, 1, 1) + contract(keys, rest, 1, 1)


def factor_of(key_rows, sketch_rows):
    hidden, rows = key_rows.shape
    rank = sketch_rows.shape[1]
    return pl.pallas_call(
        factor_kernel,
        out_shape=jax.ShapeDtypeStruct((hidden, rank), jnp.float32),
        in_specs=[pl.BlockSpec(memory_space=pl.ANY), pl.BlockSpec(memory_space=pltpu.VMEM)],
        out_specs=pl.BlockSpec(memory_space=pltpu.VMEM),
        scratch_shapes=[
            pltpu.VMEM((rank, rank + rows), jnp.float32),
            pltpu.VMEM((hidden, rows), jnp.bfloat16),
            pltpu.SemaphoreType.DMA,
        ],
        compiler_params=pltpu.CompilerParams(vmem_limit_bytes=32 * 2**20),
    )(key_rows, sketch_rows)


def solution(mesh):
    n = mesh.shape["ff"]

    def per_device(tokens, gate_weight, up_weight, test_matrix):
        key_rows, sketch_rows = keys_and_sketch(n, tokens, gate_weight.T, up_weight.T, test_matrix)
        return factor_of(key_rows, sketch_rows)

    placed = (P(("parts", "ff"), None), P(None, "ff"), P(None, "ff"), P("ff", None))
    return jax.shard_map(
        per_device, mesh=mesh, in_specs=placed, out_specs=P("ff", "parts"), check_vma=False
    )
```
